32 devices in a mesh: ctx: 16 (over z, x, core), batch: 2 (over y).
Axes of the slice: x: 2, y: 2, z: 4, core: 2. Of those that a mesh axis runs over, the one named last changes fastest.
Arguments:
- mixer_input: bfloat16 [2, 2048, 10240], P('batch', 'ctx'), may hold values from -6 to 6
- z_gate: bfloat16 [2, 2048, 8192], P('batch', 'ctx'), may hold values from -6 to 6
- time_step: bfloat16 [2, 2048, 128], P('batch', 'ctx'), may hold values from -4.5 to 0.5
- conv_weight: float32 [4, 10240], replicated, may hold values from -3 to 3
- conv_bias: float32 [10240], replicated, may hold values from -3 to 3
- decay_rate: float32 [128], replicated, may hold values from 0.000146484375 to 0.25
- skip_gain: float32 [128], replicated, may hold values from 0.3 to 1.5
- norm_gain: float32 [8192], replicated, may hold values from 0.5 to 1.5
- doc_lengths: int32 [2, 6], replicated, may hold values from 1 to 1536, 2048 in all within a row
- queries: bfloat16 [2, 2048, 4096], P('batch', 'ctx'), may hold values from -101.6466 to 101.6466
- attn_keys: bfloat16 [2, 2048, 1024], P('batch', 'ctx'), may hold values from -5 to 5
- attn_values: bfloat16 [2, 2048, 1024], P('batch', 'ctx'), may hold values from -6 to 6
Outputs:
- mixer_out: bfloat16 [2, 2048, 8192], P('batch', 'ctx')
- attn_out: bfloat16 [2, 2048, 4096], P('batch', 'ctx')
The draws below stay inside these ranges and needn't reach their ends.
Inputs may be any that keep to these rules, and one draw needn't show every extreme that they name: `doc_lengths`: each sequence's 6 lengths sum to 2048, and the longest is exactly 1536.
All inputs are finite; a program needn't handle non-finite values.
Results may differ from the reference program's by a relative error of at most 0.011.
Values may be sent and summed in bfloat16 or wider, within the bound.
A program may use at most 256 MiB of HBM per device.

```python
import math
import jax
import jax.numpy as jnp
import numpy as np
from jax import lax

HEADS = 128
HEAD_DIM = 64
STATE = 128
GROUPS = 8
QHEADS = 32
KVHEADS = 8
QDIM = 128
CONV = 4
STRETCH = 128
WINDOW = 2048
DOCS = 6
TOK_DEV = 128
SEQS = 2
SEQ_LEN = 2048
MOST = 1536


def draw_time_step(key, part):
    element_key, block_key = jax.random.split(jax.random.fold_in(key, 3))
    element = jax.random.uniform(element_key, (SEQS, SEQ_LEN, HEADS), jnp.float32, -3.5, -0.5)
    offsets = jax.random.uniform(block_key, (SEQS, SEQ_LEN // TOK_DEV, 1, HEADS), jnp.float32, -1.0, 1.0)
    shifted = element.reshape(SEQS, SEQ_LEN // TOK_DEV, TOK_DEV, HEADS) + offsets
    return shifted.reshape(SEQS, SEQ_LEN, HEADS).astype(jnp.bfloat16)


def draw_decay_rate(key, part):
    mix_key = jax.random.fold_in(jax.random.fold_in(key, 5), 0)
    lowest = math.log(0.3 / SEQ_LEN)
    fraction = jax.random.uniform(mix_key, (HEADS,), jnp.float32)
    return jnp.exp(lowest + fraction * (math.log(0.25) - lowest)).astype(jnp.float32)


def attention_pair(key):
    base_key = jax.random.fold_in(key, 11)
    key_key, query_key = jax.random.split(base_key)
    keys_drawn = jnp.clip(jax.random.normal(key_key, (SEQS, SEQ_LEN, KVHEADS, QDIM), jnp.float32), -5.0, 5.0)
    queries_drawn = jnp.clip(jax.random.normal(query_key, (SEQS, SEQ_LEN, KVHEADS, QHEADS // KVHEADS, QDIM), jnp.float32), -5.0, 5.0)
    return (keys_drawn.reshape(SEQS, SEQ_LEN, KVHEADS * QDIM), queries_drawn.reshape(SEQS, SEQ_LEN, QHEADS * QDIM))


def draw_queries(key, part):
    return attention_pair(key)[1].astype(jnp.bfloat16)


def draw_attn_keys(key, part):
    return attention_pair(key)[0].astype(jnp.bfloat16)


def block_levels(rng, extent, cuts, least, high):
    loudness = 1.0
    for dim, parts in cuts:
        draws = jax.random.uniform(jax.random.fold_in(jax.random.fold_in(rng, 6), dim), (parts,), jnp.float32, least / len(cuts), high / len(cuts))
        loudness = loudness * jnp.repeat(jnp.exp(draws), extent[dim] // parts).reshape((-1,) + (1,) * (len(extent) - 1 - dim))
    return loudness


def split_up(count, total, most, lean):
    weights = [(1 << 20) // math.isqrt(rank ** lean) + 1 for rank in range(2, count + 1)]
    surplus, holding = total - most - (count - 1), [1] * (count - 1)
    while surplus > 0:
        free = [i for i in range(count - 1) if holding[i] < most]
        pool, left = sum([weights[i] for i in free]), surplus
        for i in free:
            extra = min(most - holding[i], max(1, left * weights[i] // pool), surplus)
            holding[i] = holding[i] + extra
            surplus = surplus - extra
    return np.array([most] + holding)


def ragged_sizes(stream_key, number_of, total, reach, lean):
    if number_of == 2:
        one = jax.random.randint(stream_key, (), max(1, total - reach), min(reach, total - 1) + 1)
        return jnp.stack([one, total - one])
    sizes = jnp.asarray(split_up(number_of, total, reach, lean), jnp.int32)
    couples = (number_of - 1) // 2
    giver, receiver = sizes[1:1 + 2 * couples:2], sizes[2:2 + 2 * couples:2]
    slack = jnp.minimum(giver - 1, reach - receiver)
    moved = jax.random.randint(jax.random.fold_in(stream_key, 1), (couples,), 0, 1 << 20) % (slack + 1)
    sizes = sizes.at[1:1 + 2 * couples:2].set(giver - moved).at[2:2 + 2 * couples:2].set(receiver + moved)
    return sizes[jax.random.permutation(jax.random.fold_in(stream_key, 2), number_of)]


def bell_draw(rng, shape, scale, most, cuts=(), held_as=jnp.bfloat16):
    loudness = block_levels(rng, shape, cuts, -0.22, 0.18) if cuts else 1.0
    values = jax.random.normal(rng, shape, jnp.float32) * scale * loudness
    return jnp.minimum(jnp.maximum(values, -most), most).astype(held_as)


def setup_inputs(seed: int = 0) -> dict:
    splits = jax.random.split(jax.random.key(seed), 13)
    return {
        "mixer_input": bell_draw(splits[0], (SEQS, SEQ_LEN, HEADS * HEAD_DIM + 2 * GROUPS * STATE), 1.0, 6.0, ((0, 2), (1, 16))),
        "z_gate": bell_draw(splits[1], (SEQS, SEQ_LEN, HEADS * HEAD_DIM), 1.0, 6.0, ((0, 2), (1, 16))),
        "time_step": draw_time_step(jax.random.fold_in(splits[12], 71), 0),
        "conv_weight": bell_draw(splits[3], (CONV, HEADS * HEAD_DIM + 2 * GROUPS * STATE), CONV ** -0.5, 3.0, (), jnp.float32),
        "conv_bias": bell_draw(splits[4], (HEADS * HEAD_DIM + 2 * GROUPS * STATE,), 0.5, 3.0, (), jnp.float32),
        "decay_rate": draw_decay_rate(jax.random.fold_in(splits[12], 71), 0),
        "skip_gain": jnp.clip(jax.random.uniform(splits[6], (HEADS,), jnp.float32, 0.3, 1.5), 0.3, 1.5),
        "norm_gain": jnp.clip(1.0 + 0.1 * jax.random.normal(splits[7], (HEADS * HEAD_DIM,), jnp.float32), 0.5, 1.5),
        "doc_lengths": jax.vmap(lambda own: ragged_sizes(own, DOCS, SEQ_LEN, MOST, 2))(jax.random.split(splits[8], SEQS)).reshape((SEQS, DOCS)).astype(jnp.int32),
        "queries": draw_queries(jax.random.fold_in(splits[12], 71), 0),
        "attn_keys": draw_attn_keys(jax.random.fold_in(splits[12], 71), 0),
        "attn_values": bell_draw(splits[11], (SEQS, SEQ_LEN, KVHEADS * QDIM), 1.0, 6.0, ((0, 2), (1, 16))),
    }


EPSILON = 1e-05
NEGATIVE = -1e+30

def product(pattern, first_op, second_op):
    return jnp.einsum(pattern, first_op.astype(jnp.float32), second_op.astype(jnp.float32), precision=lax.Precision.HIGHEST)

def segment_ids(doc_lengths, positions):
    endings = jnp.cumsum(doc_lengths, axis=-1, dtype=jnp.int32)
    starting = endings - doc_lengths
    return lax.optimization_barrier(jnp.sum((starting[:, None, :] <= positions[None, :, None]).astype(jnp.int32), axis=-1, dtype=jnp.int32)) - 1

def causal_conv(inputs, conv_weight, conv_bias, segments, rim_rows, rim_segments):
    padded = jnp.concatenate([rim_rows, inputs], axis=1).astype(jnp.float32)
    padded_seg = jnp.concatenate([rim_segments, segments], axis=1)
    length = inputs.shape[1]
    kernel_taps = conv_weight.shape[0]
    summed = jnp.zeros(inputs.shape, jnp.float32) + conv_bias
    for offset in range(kernel_taps):
        window_rows = padded[:, offset:offset + length]
        matches = (padded_seg[:, offset:offset + length] == segments)[..., None]
        summed = summed + jnp.where(matches, window_rows * conv_weight[offset], 0.0)
    return jax.nn.silu(summed).astype(jnp.bfloat16)

def ssd_block(carried_in, pieces, decay_rates, skip_gains):
    state_now, prev_seg = carried_in
    head_inputs, step_sizes, input_proj, output_proj, segments = pieces
    log_decay = jnp.cumsum(-step_sizes * decay_rates, axis=1)
    block_len = segments.shape[1]
    position = jnp.arange(block_len, dtype=jnp.int32)
    related = (segments[:, :, None] == segments[:, None, :]) & (position[:, None] >= position[None, :])
    spread = log_decay[:, :, None] - log_decay[:, None, :]
    decays = jnp.where(related[..., None, None], jnp.exp(jnp.minimum(spread, 0.0)), 0.0)
    scores = product('sqgn,skgn->sqkg', output_proj, input_proj)
    weights = (scores[..., None] * decays * step_sizes[:, None]).astype(jnp.bfloat16)
    inner_part = product('sqkgr,skgrp->sqgrp', weights, head_inputs)
    carried = product('sqgn,sgrnp->sqgrp', output_proj, state_now)
    keep_rows = (segments == prev_seg[:, None])[:, :, None, None]
    between = jnp.where(keep_rows, jnp.exp(log_decay), 0.0)[..., None] * carried
    outputs = inner_part + between + skip_gains[..., None] * head_inputs.astype(jnp.float32)
    last_seg = segments[:, -1]
    trailing = jnp.where((segments == last_seg[:, None])[:, :, None, None], jnp.exp(log_decay[:, -1:] - log_decay) * step_sizes, 0.0)
    fresh_state = product('sqgn,sqgrp->sgrnp', input_proj, trailing[..., None] * head_inputs.astype(jnp.float32))
    through = jnp.where((last_seg == prev_seg)[:, None, None], jnp.exp(log_decay[:, -1]), 0.0)
    return ((through[..., None, None] * state_now + fresh_state, last_seg), outputs.astype(jnp.bfloat16))

def run_blocks(head_inputs, step_sizes, input_proj, output_proj, segments, decay_rates, skip_gains, block_len):
    num_seqs, length = segments.shape
    state_zero = jnp.zeros((num_seqs,) + head_inputs.shape[2:4] + (input_proj.shape[-1], head_inputs.shape[-1]), jnp.float32)
    prev_zero = jnp.full((num_seqs,), -1, jnp.int32)

    def advance(carried_in, block_index):
        block_start = block_index * block_len
        pieces = tuple((lax.dynamic_slice_in_dim(array_in, block_start, block_len, 1) for array_in in (head_inputs, step_sizes, input_proj, output_proj, segments)))
        return ssd_block(carried_in, pieces, decay_rates, skip_gains)
    final_carry, outputs = lax.scan(advance, (state_zero, prev_zero), jnp.arange(length // block_len, dtype=jnp.int32))
    return jnp.moveaxis(outputs, 0, 1).reshape(head_inputs.shape)

def reference(mixer_input, z_gate, time_step, conv_weight, conv_bias, decay_rate, skip_gain, norm_gain, doc_lengths, queries, attn_keys, attn_values):
    inner_width = HEADS * HEAD_DIM
    proj_width = GROUPS * STATE
    per_group = HEADS // GROUPS
    segments = segment_ids(doc_lengths, jnp.arange(SEQ_LEN, dtype=jnp.int32))

    def convolve(operands):
        sequence, seq_segments = operands
        rim_rows = jnp.zeros((1, CONV - 1, sequence.shape[-1]), jnp.bfloat16)
        rim_segments = jnp.full((1, CONV - 1), -1, jnp.int32)
        return causal_conv(sequence[None], conv_weight, conv_bias, seq_segments[None], rim_rows, rim_segments)[0]
    activated = lax.map(convolve, (mixer_input, segments))
    head_inputs = activated[:, :, :inner_width].reshape(SEQS, SEQ_LEN, GROUPS, per_group, HEAD_DIM)
    input_proj = activated[:, :, inner_width:inner_width + proj_width].reshape(SEQS, SEQ_LEN, GROUPS, STATE)
    output_proj = activated[:, :, inner_width + proj_width:].reshape(SEQS, SEQ_LEN, GROUPS, STATE)
    step_sizes = jax.nn.softplus(time_step.astype(jnp.float32)).reshape(SEQS, SEQ_LEN, GROUPS, per_group)
    mixed = run_blocks(head_inputs, step_sizes, input_proj, output_proj, segments, decay_rate.reshape(GROUPS, per_group), skip_gain.reshape(GROUPS, per_group), STRETCH)
    mixed = mixed.reshape(SEQS, SEQ_LEN, inner_width)

    def normalize(operands):
        mixed_seq, gate_seq = operands
        gated = mixed_seq.astype(jnp.float32) * jax.nn.silu(gate_seq.astype(jnp.float32))
        grouped = gated.reshape(SEQ_LEN, GROUPS, inner_width // GROUPS)
        scaling = lax.rsqrt(lax.optimization_barrier(jnp.mean(grouped * grouped, axis=-1, keepdims=True)) + EPSILON)
        return ((grouped * scaling).reshape(SEQ_LEN, inner_width) * norm_gain).astype(jnp.bfloat16)
    mixer_out = lax.map(normalize, (mixed, z_gate))
    block_rows = 512 if SEQ_LEN % 512 == 0 else SEQ_LEN
    group_size = QHEADS // KVHEADS
    key_span = block_rows + WINDOW - 1
    scaling = QDIM ** (-0.5)

    def attend_sequence(operands):
        query_seq, key_seq, value_seq, seq_segments = operands
        keys_padded = jnp.concatenate([jnp.zeros((WINDOW - 1, KVHEADS * QDIM), jnp.bfloat16), key_seq], axis=0).reshape(-1, KVHEADS, QDIM)
        values_padded = jnp.concatenate([jnp.zeros((WINDOW - 1, KVHEADS * QDIM), jnp.bfloat16), value_seq], axis=0).reshape(-1, KVHEADS, QDIM)
        segs_padded = jnp.concatenate([jnp.full((WINDOW - 1,), -1, jnp.int32), seq_segments], axis=0)

        def attend_block(block_index):
            query_start = block_index * block_rows
            query_block = lax.dynamic_slice_in_dim(query_seq, query_start, block_rows, 0).reshape(block_rows, KVHEADS, group_size, QDIM)
            key_block = lax.dynamic_slice_in_dim(keys_padded, query_start, key_span, 0)
            value_block = lax.dynamic_slice_in_dim(values_padded, query_start, key_span, 0)
            key_segs = lax.dynamic_slice_in_dim(segs_padded, query_start, key_span, 0)
            query_segs = lax.dynamic_slice_in_dim(seq_segments, query_start, block_rows, 0)
            query_pos = query_start + jnp.arange(block_rows, dtype=jnp.int32)
            key_pos = query_start - (WINDOW - 1) + jnp.arange(key_span, dtype=jnp.int32)
            visible = (key_segs[None, :] == query_segs[:, None]) & (key_pos[None, :] <= query_pos[:, None]) & (query_pos[:, None] - key_pos[None, :] < WINDOW)
            scores = product('qkgd,rkd->kgqr', query_block, key_block) * scaling
            masked = jnp.where(visible, scores, NEGATIVE)
            highest = lax.optimization_barrier(jnp.max(masked, axis=-1, keepdims=True))
            numerators = jnp.where(visible, jnp.exp(masked - highest), 0.0)
            totals = lax.optimization_barrier(jnp.sum(numerators, axis=-1))
            summed = product('kgqr,rkd->qkgd', numerators.astype(jnp.bfloat16), value_block)
            return (summed / jnp.moveaxis(totals, -1, 0)[..., None]).reshape(block_rows, QHEADS * QDIM).astype(jnp.bfloat16)
        blocks = lax.map(attend_block, jnp.arange(SEQ_LEN // block_rows, dtype=jnp.int32))
        return blocks.reshape(SEQ_LEN, QHEADS * QDIM)
    attn_out = lax.map(attend_sequence, (queries, attn_keys, attn_values, segments))
    return (mixer_out, attn_out)
```

```python
import functools

import jax
import jax.numpy as jnp
from jax import lax
from jax.experimental import pallas as pl
from jax.experimental.pallas import tpu as pltpu
from jax.sharding import PartitionSpec as P

HEADS = 128
HEAD_DIM = 64
STATE = 128
GROUPS = 8
QHEADS = 32
KVHEADS = 8
QDIM = 128
PER_GROUP = HEADS // GROUPS
GROUP_WIDTH = PER_GROUP * HEAD_DIM
RIM = 16

EPSILON = 1e-05
NEGATIVE = -1e30
F32 = jnp.float32
BF16 = jnp.bfloat16
MESH = pl.DeviceIdType.MESH


def start_of(info_ref, positions, docs):
    start = jnp.zeros_like(positions)
    for doc in range(1, docs):
        first = info_ref[1 + doc]
        start = jnp.where(positions >= first, first, start)
    return start


def log_decays(step_ref, rate_ref, rows):
    steps = jax.nn.softplus(step_ref[...].astype(F32))
    fall = -steps * rate_ref[...]
    lower = (
        lax.broadcasted_iota(jnp.int32, (rows, rows), 0)
        >= lax.broadcasted_iota(jnp.int32, (rows, rows), 1)
    ).astype(F32)
    return steps, jnp.dot(
        lower, fall, precision=lax.Precision.HIGHEST, preferred_element_type=F32
    )


def spread_heads(per_head):
    high = per_head.astype(BF16)
    low = (per_head - high.astype(F32)).astype(BF16)
    both = jnp.concatenate([high, low], axis=1)
    row = lax.broadcasted_iota(jnp.int32, (2 * PER_GROUP, GROUP_WIDTH), 0)
    col = lax.broadcasted_iota(jnp.int32, (2 * PER_GROUP, GROUP_WIDTH), 1)
    own = (lax.rem(row, PER_GROUP) == lax.div(col, HEAD_DIM)).astype(BF16)
    return jnp.dot(both, own, preferred_element_type=F32)


def conv_silu(in_ref, rim_ref, weight_ref, bias_ref, pad_ref, same):
    rows, width = in_ref.shape
    pad_ref[0:8, 0:width] = rim_ref[8:16, :].astype(F32)
    pad_ref[8 : 8 + rows, 0:width] = in_ref[...].astype(F32)
    taps = weight_ref.shape[0]
    summed = pad_ref[8 : 8 + rows, 0:width] * weight_ref[taps - 1 : taps, :] + bias_ref[...]
    for back in range(1, taps):
        window = pad_ref[8 - back : 8 - back + rows, 0:width]
        tap = weight_ref[taps - 1 - back : taps - back, :]
        summed = summed + jnp.where(same[back - 1], window * tap, 0.0)
    return (summed * jax.nn.sigmoid(summed)).astype(BF16)


def fresh_kernel(
    docs,
    info_ref,
    x_ref, b_ref, c_ref,
    rim_x_ref, rim_b_ref, rim_c_ref,
    w_x_ref, w_b_ref, w_c_ref,
    o_x_ref, o_b_ref, o_c_ref,
    step_ref, rate_ref,
    act_ref, proj_ref, fresh_ref, through_ref,
    pad_ref, trail_ref, last_ref,
):
    rows = x_ref.shape[0]
    group = pl.program_id(0)
    base = info_ref[0]
    pos = base + lax.broadcasted_iota(jnp.int32, (rows, 1), 0)
    start = start_of(info_ref, pos, docs)

    @pl.when(group == 0)
    def _():
        steps, decay = log_decays(step_ref, rate_ref, rows)
        last_pos = jnp.full((rows, 1), base + rows - 1, jnp.int32)
        last_start = start_of(info_ref, last_pos, docs)
        final = decay[rows - 1 : rows, :]
        trail = jnp.where(pos >= last_start, jnp.exp(final - decay) * steps, 0.0)
        carry = jnp.where(
            last_start[0:8] < base, jnp.exp(jnp.broadcast_to(final, (8, HEADS))), 0.0
        )
        for k in range(GROUPS):
            trail_ref[k] = trail[:, k * PER_GROUP : (k + 1) * PER_GROUP]
            last_ref[k] = carry[:, k * PER_GROUP : (k + 1) * PER_GROUP]

    same = [pos - back >= start for back in range(1, w_x_ref.shape[0])]
    x = conv_silu(x_ref, rim_x_ref, w_x_ref, o_x_ref, pad_ref, same)
    b = conv_silu(b_ref, rim_b_ref, w_b_ref, o_b_ref, pad_ref, same)
    c = conv_silu(c_ref, rim_c_ref, w_c_ref, o_c_ref, pad_ref, same)
    act_ref[...] = x
    proj_ref[0, 0] = b
    proj_ref[0, 1] = c
    scaled = (x.astype(F32) * spread_heads(trail_ref[group])).astype(BF16)
    fresh_ref[0] = lax.dot_general(
        b, scaled, (((0,), (0,)), ((), ())), preferred_element_type=F32
    ).astype(BF16)
    through_ref[0] = spread_heads(last_ref[group])


def chain_kernel(n, fresh_ref, through_ref, before_ref, got, sent, send_sem, recv_sem):
    rank = lax.axis_index("ctx")
    right, left = lax.rem(rank + 1, n), lax.rem(rank + n - 1, n)
    barrier = pltpu.get_barrier_semaphore()
    for neighbour in (left, right):
        pl.semaphore_signal(barrier, inc=1, device_id={"ctx": neighbour}, device_id_type=MESH)
    pl.semaphore_wait(barrier, 2)
    pieces = got.shape[0]
    splits = pieces // GROUPS
    width = got.shape[2]

    def hand_on(piece):
        return pltpu.make_async_remote_copy(
            src_ref=sent.at[piece],
            dst_ref=got.at[piece],
            send_sem=send_sem.at[piece],
            recv_sem=recv_sem.at[piece],
            device_id={"ctx": right},
            device_id_type=MESH,
        )

    @pl.when(rank == 0)
    def _():
        for piece in range(pieces):
            cols = slice((piece % splits) * width, (piece % splits + 1) * width)
            sent[piece] = fresh_ref[piece // splits, :, cols]
            hand_on(piece).start()
        before_ref[...] = jnp.zeros_like(before_ref)

    @pl.when(rank > 0)
    def _():
        for piece in range(pieces):
            group, cols = piece // splits, slice(
                (piece % splits) * width, (piece % splits + 1) * width
            )
            hand_on(piece).wait_recv()

            @pl.when(rank < n - 1)
            def _():
                sent[piece] = (
                    through_ref[group, 0:1, cols] * got[piece].astype(F32)
                    + fresh_ref[group, :, cols].astype(F32)
                ).astype(BF16)
                hand_on(piece).start()

            before_ref[group, :, cols] = got[piece]

    @pl.when(rank < n - 1)
    def _():
        for piece in range(pieces):
            hand_on(piece).wait_send()


def mix_kernel(
    docs,
    info_ref,
    x_ref, proj_ref, before_ref, z_ref, gain_ref, skip_ref, step_ref, rate_ref,
    out_ref,
    decay_ref, late_ref, row_ref,
):
    rows = x_ref.shape[0]
    group = pl.program_id(0)
    base = info_ref[0]
    pos = base + lax.broadcasted_iota(jnp.int32, (rows, 1), 0)
    start = start_of(info_ref, pos, docs)

    @pl.when(group == 0)
    def _():
        steps, decay = log_decays(step_ref, rate_ref, rows)
        late = jnp.where(start < base, jnp.exp(decay), 0.0)
        for k in range(GROUPS):
            decay_ref[k] = decay[:, k * PER_GROUP : (k + 1) * PER_GROUP]
            late_ref[k] = late[:, k * PER_GROUP : (k + 1) * PER_GROUP]
        row_ref[...] = (decay - jnp.log(steps)).T

    x = x_ref[...]
    b, c = proj_ref[0, 0], proj_ref[0, 1]
    key_pos = base + lax.broadcasted_iota(jnp.int32, (rows, rows), 1)
    related = (key_pos <= pos) & (key_pos >= start)
    scores = lax.dot_general(c, b, (((1,), (1,)), ((), ())), preferred_element_type=F32)
    scores = jnp.where(related, scores, 0.0)
    columns = decay_ref[group]
    lines = row_ref[pl.ds(pl.multiple_of(group * PER_GROUP, PER_GROUP), PER_GROUP), :]
    lane = lax.broadcasted_iota(jnp.int32, (rows, 2 * HEAD_DIM), 1)
    first = lane < HEAD_DIM
    parts = []
    for pair in range(PER_GROUP // 2):
        weights = []
        for head in (2 * pair, 2 * pair + 1):
            weights.append(
                (
                    scores * jnp.exp(columns[:, head : head + 1] - lines[head : head + 1, :])
                ).astype(BF16)
            )
        own = x[:, pair * 2 * HEAD_DIM : (pair + 1) * 2 * HEAD_DIM]
        zero = jnp.zeros_like(own)
        stacked = jnp.concatenate([jnp.where(first, own, zero), jnp.where(first, zero, own)], axis=0)
        parts.append(
            jnp.dot(jnp.concatenate(weights, axis=1), stacked, preferred_element_type=F32)
        )
    inner = jnp.concatenate(parts, axis=1)
    carried = jnp.dot(c, before_ref[0], preferred_element_type=F32)
    mixed = inner + carried * spread_heads(late_ref[group]) + skip_ref[...] * x.astype(F32)
    z = z_ref[...].astype(F32)
    gated = mixed * (z * jax.nn.sigmoid(z))
    scaling = lax.rsqrt(jnp.mean(gated * gated, axis=1, keepdims=True) + EPSILON)
    out_ref[...] = (gated * scaling * gain_ref[...]).astype(BF16)


def attend_kernel(docs, step_rows, info_ref, q_ref, k_ref, v_ref, out_ref):
    rows = q_ref.shape[0]
    group_size = q_ref.shape[1] // QDIM
    base = info_ref[0]
    q = jnp.concatenate([q_ref[:, i * QDIM : (i + 1) * QDIM] for i in range(group_size)], axis=0)
    tall = rows * group_size
    pos = base + lax.rem(lax.broadcasted_iota(jnp.int32, (tall, 1), 0), rows)
    start = start_of(info_ref, pos, docs)
    earliest = jnp.int32(0)
    for doc in range(1, docs):
        earliest = jnp.where(base >= info_ref[1 + doc], info_ref[1 + doc], earliest)
    scaling = QDIM ** (-0.5)

    def step(block, carry):
        high, accum = carry
        offset = pl.multiple_of(block * step_rows, step_rows)
        keys = k_ref[pl.ds(offset, step_rows), :]
        values = v_ref[pl.ds(offset, step_rows), :]
        scores = (
            lax.dot_general(q, keys, (((1,), (1,)), ((), ())), preferred_element_type=F32)
            * scaling
        )
        key_pos = offset + lax.broadcasted_iota(jnp.int32, (tall, step_rows), 1)
        visible = (key_pos <= pos) & (key_pos >= start)
        masked = jnp.where(visible, scores, NEGATIVE)
        high_next = jnp.maximum(high, jnp.max(masked, axis=1, keepdims=True))
        numerators = jnp.where(visible, jnp.exp(masked - high_next), 0.0)
        fading = jnp.exp(high - high_next)
        wide = jnp.concatenate([values, jnp.ones_like(values)], axis=1)
        accum_next = accum * fading + jnp.dot(
            numerators.astype(BF16), wide, preferred_element_type=F32
        )
        return high_next, accum_next

    first_block = lax.div(earliest, step_rows)
    last_block = lax.div(base + rows - 1, step_rows) + 1
    high, accum = lax.fori_loop(
        first_block,
        last_block,
        step,
        (jnp.full((tall, 1), NEGATIVE, F32), jnp.zeros((tall, 2 * QDIM), F32)),
    )
    result = (accum[:, :QDIM] / accum[:, QDIM:]).astype(BF16)
    for i in range(group_size):
        out_ref[:, i * QDIM : (i + 1) * QDIM] = result[i * rows : (i + 1) * rows, :]


def params(limit, **more):
    return pltpu.CompilerParams(vmem_limit_bytes=limit * 2**20, **more)


def on_device(
    mixer_input,
    z_gate,
    time_step,
    conv_weight,
    conv_bias,
    decay_rate,
    skip_gain,
    norm_gain,
    doc_lengths,
    queries,
    attn_keys,
    attn_values,
):
    rows = mixer_input.shape[1]
    width = mixer_input.shape[2]
    inner_width = HEADS * HEAD_DIM
    docs = doc_lengths.shape[1]
    taps = conv_weight.shape[0]
    n = lax.axis_size("ctx")
    rank = lax.axis_index("ctx")
    keys = lax.all_gather(attn_keys[0], "ctx", axis=0, tiled=True)
    values = lax.all_gather(attn_values[0], "ctx", axis=0, tiled=True)
    rim = lax.ppermute(
        mixer_input[0, rows - RIM :, :], "ctx", [(i, i + 1) for i in range(n - 1)]
    )
    lengths = lax.dynamic_slice_in_dim(doc_lengths, lax.axis_index("batch"), 1, 0)[0]
    info = jnp.concatenate([(rank * rows).astype(jnp.int32)[None], jnp.cumsum(lengths) - lengths])
    rates = decay_rate[None]
    bias = conv_bias[None]
    skips = jnp.repeat(skip_gain, HEAD_DIM)[None]
    first_b = inner_width // STATE
    first_c = first_b + GROUPS
    smem = pl.BlockSpec(memory_space=pltpu.SMEM)

    def wide(height):
        return pl.BlockSpec((height, GROUP_WIDTH), lambda g: (0, g))

    def narrow(height, first):
        return pl.BlockSpec((height, STATE), lambda g: (0, first + g))

    def trio(height):
        return [wide(height), narrow(height, first_b), narrow(height, first_c)]

    whole = pl.BlockSpec((rows, HEADS), lambda g: (0, 0))
    rate_spec = pl.BlockSpec((1, HEADS), lambda g: (0, 0))
    per_group = lambda *shape: pl.BlockSpec((1,) + shape, lambda g: (g,) + (0,) * len(shape))
    inputs = mixer_input[0]
    act, proj, fresh, through = pl.pallas_call(
        functools.partial(fresh_kernel, docs),
        grid=(GROUPS,),
        in_specs=[smem] + trio(rows) + trio(RIM) + trio(taps) + trio(1) + [whole, rate_spec],
        out_specs=[
            wide(rows),
            per_group(2, rows, STATE),
            per_group(STATE, GROUP_WIDTH),
            per_group(8, GROUP_WIDTH),
        ],
        out_shape=[
            jax.ShapeDtypeStruct((rows, inner_width), BF16),
            jax.ShapeDtypeStruct((GROUPS, 2, rows, STATE), BF16),
            jax.ShapeDtypeStruct((GROUPS, STATE, GROUP_WIDTH), BF16),
            jax.ShapeDtypeStruct((GROUPS, 8, GROUP_WIDTH), F32),
        ],
        scratch_shapes=[
            pltpu.VMEM((8 + rows, GROUP_WIDTH), F32),
            pltpu.VMEM((GROUPS, rows, PER_GROUP), F32),
            pltpu.VMEM((GROUPS, 8, PER_GROUP), F32),
        ],
        compiler_params=params(24),
        cost_estimate=pl.CostEstimate(
            flops=6 * 10**8, bytes_accessed=8 * 10**6, transcendentals=10**6
        ),
        name="fresh_states",
    )(
        info,
        inputs, inputs, inputs,
        rim, rim, rim,
        conv_weight, conv_weight, conv_weight,
        bias, bias, bias,
        time_step[0],
        rates,
    )

    pieces = 2 * GROUPS
    piece_width = GROUPS * GROUP_WIDTH // pieces
    vmem = pl.BlockSpec(memory_space=pltpu.VMEM)
    before = pl.pallas_call(
        functools.partial(chain_kernel, n),
        in_specs=[vmem, vmem],
        out_specs=vmem,
        out_shape=jax.ShapeDtypeStruct((GROUPS, STATE, GROUP_WIDTH), BF16),
        scratch_shapes=[
            pltpu.VMEM((pieces, STATE, piece_width), BF16),
            pltpu.VMEM((pieces, STATE, piece_width), BF16),
            pltpu.SemaphoreType.DMA((pieces,)),
            pltpu.SemaphoreType.DMA((pieces,)),
        ],
        compiler_params=params(24, collective_id=0, has_side_effects=True),
        cost_estimate=pl.CostEstimate(
            flops=10**7, bytes_accessed=2 * 10**8, transcendentals=0
        ),
        name="hand_on_states",
    )(fresh, through)

    mixer_out = pl.pallas_call(
        functools.partial(mix_kernel, docs),
        grid=(GROUPS,),
        in_specs=[
            smem,
            wide(rows),
            per_group(2, rows, STATE),
            per_group(STATE, GROUP_WIDTH),
            wide(rows),
            wide(1),
            wide(1),
            whole,
            rate_spec,
        ],
        out_specs=wide(rows),
        out_shape=jax.ShapeDtypeStruct((rows, inner_width), BF16),
        scratch_shapes=[
            pltpu.VMEM((GROUPS, rows, PER_GROUP), F32),
            pltpu.VMEM((GROUPS, rows, PER_GROUP), F32),
            pltpu.VMEM((HEADS, rows), F32),
        ],
        compiler_params=params(24),
        cost_estimate=pl.CostEstimate(
            flops=10**9, bytes_accessed=10**7, transcendentals=4 * 10**6
        ),
        name="mix_heads",
    )(info, act, proj, before, z_gate[0], norm_gain[None], skips, time_step[0], rates)

    seq_len = keys.shape[0]
    q_width = queries.shape[2] // KVHEADS
    step_rows = 256
    attn_out = pl.pallas_call(
        functools.partial(attend_kernel, docs, step_rows),
        grid=(KVHEADS,),
        in_specs=[
            smem,
            pl.BlockSpec((rows, q_width), lambda g: (0, g)),
            pl.BlockSpec((seq_len, QDIM), lambda g: (0, g)),
            pl.BlockSpec((seq_len, QDIM), lambda g: (0, g)),
        ],
        out_specs=pl.BlockSpec((rows, q_width), lambda g: (0, g)),
        out_shape=jax.ShapeDtypeStruct((rows, QHEADS * QDIM), BF16),
        compiler_params=params(24),
        cost_estimate=pl.CostEstimate(
            flops=4 * 10**9, bytes_accessed=10**7, transcendentals=8 * 10**6
        ),
        name="attend",
    )(info, queries[0], keys, values)
    return (mixer_out[None], attn_out[None])


def solution(mesh):
    spread = P("batch", "ctx", None)
    placed = (spread,) * 3 + (P(),) * 6 + (spread,) * 3
    return jax.shard_map(
        on_device,
        mesh=mesh,
        in_specs=placed,
        out_specs=(spread, spread),
        check_vma=False,
    )
```

```python
import functools

import jax
import jax.numpy as jnp
from jax import lax
from jax.experimental import pallas as pl
from jax.experimental.pallas import tpu as pltpu
from jax.sharding import PartitionSpec as P

HEADS = 128
HEAD_DIM = 64
STATE = 128
GROUPS = 8
QHEADS = 32
KVHEADS = 8
QDIM = 128
PER_GROUP = HEADS // GROUPS
GROUP_WIDTH = PER_GROUP * HEAD_DIM
RIM = 16
MOST = 1536
PLANE = 4

EPSILON = 1e-05
NEGATIVE = -1e30
F32 = jnp.float32
BF16 = jnp.bfloat16
MESH = pl.DeviceIdType.MESH


def start_of(info_ref, positions, docs):
    start = jnp.zeros_like(positions)
    for doc in range(1, docs):
        first = info_ref[1 + doc]
        start = jnp.where(positions >= first, first, start)
    return start


def log_decays(step_ref, rate_ref, rows):
    steps = jax.nn.softplus(step_ref[...].astype(F32))
    fall = -steps * rate_ref[...]
    lower = (
        lax.broadcasted_iota(jnp.int32, (rows, rows), 0)
        >= lax.broadcasted_iota(jnp.int32, (rows, rows), 1)
    ).astype(F32)
    return steps, jnp.dot(
        lower, fall, precision=lax.Precision.HIGHEST, preferred_element_type=F32
    )


def spread_heads(per_head):
    high = per_head.astype(BF16)
    low = (per_head - high.astype(F32)).astype(BF16)
    both = jnp.concatenate([high, low], axis=1)
    row = lax.broadcasted_iota(jnp.int32, (2 * PER_GROUP, GROUP_WIDTH), 0)
    col = lax.broadcasted_iota(jnp.int32, (2 * PER_GROUP, GROUP_WIDTH), 1)
    own = (lax.rem(row, PER_GROUP) == lax.div(col, HEAD_DIM)).astype(BF16)
    return jnp.dot(both, own, preferred_element_type=F32)


def conv_silu(in_ref, rim_ref, weight_ref, bias_ref, pad_ref, same):
    rows, width = in_ref.shape
    pad_ref[0:8, 0:width] = rim_ref[8:16, :].astype(F32)
    pad_ref[8 : 8 + rows, 0:width] = in_ref[...].astype(F32)
    taps = weight_ref.shape[0]
    summed = pad_ref[8 : 8 + rows, 0:width] * weight_ref[taps - 1 : taps, :] + bias_ref[...]
    for back in range(1, taps):
        window = pad_ref[8 - back : 8 - back + rows, 0:width]
        tap = weight_ref[taps - 1 - back : taps - back, :]
        summed = summed + jnp.where(same[back - 1], window * tap, 0.0)
    return (summed * jax.nn.sigmoid(summed)).astype(BF16)


def fresh_kernel(
    docs,
    info_ref,
    x_ref, b_ref, c_ref,
    rim_x_ref, rim_b_ref, rim_c_ref,
    w_x_ref, w_b_ref, w_c_ref,
    o_x_ref, o_b_ref, o_c_ref,
    step_ref, rate_ref,
    act_ref, proj_ref, fresh_ref, through_ref,
    pad_ref, trail_ref, last_ref,
):
    rows = x_ref.shape[0]
    group = pl.program_id(0)
    base = info_ref[0]
    pos = base + lax.broadcasted_iota(jnp.int32, (rows, 1), 0)
    start = start_of(info_ref, pos, docs)

    @pl.when(group == 0)
    def _():
        steps, decay = log_decays(step_ref, rate_ref, rows)
        last_pos = jnp.full((rows, 1), base + rows - 1, jnp.int32)
        last_start = start_of(info_ref, last_pos, docs)
        final = decay[rows - 1 : rows, :]
        trail = jnp.where(pos >= last_start, jnp.exp(final - decay) * steps, 0.0)
        carry = jnp.where(
            last_start[0:8] < base, jnp.exp(jnp.broadcast_to(final, (8, HEADS))), 0.0
        )
        for k in range(GROUPS):
            trail_ref[k] = trail[:, k * PER_GROUP : (k + 1) * PER_GROUP]
            last_ref[k] = carry[:, k * PER_GROUP : (k + 1) * PER_GROUP]

    same = [pos - back >= start for back in range(1, w_x_ref.shape[0])]
    x = conv_silu(x_ref, rim_x_ref, w_x_ref, o_x_ref, pad_ref, same)
    b = conv_silu(b_ref, rim_b_ref, w_b_ref, o_b_ref, pad_ref, same)
    c = conv_silu(c_ref, rim_c_ref, w_c_ref, o_c_ref, pad_ref, same)
    act_ref[...] = x
    proj_ref[0, 0] = b
    proj_ref[0, 1] = c
    scaled = (x.astype(F32) * spread_heads(trail_ref[group])).astype(BF16)
    fresh_ref[0] = lax.dot_general(
        b, scaled, (((0,), (0,)), ((), ())), preferred_element_type=F32
    ).astype(BF16)
    through_ref[0] = spread_heads(last_ref[group])


def chain_kernel(
    n,
    reach,
    fresh_ref, through_ref, kv_ref,
    before_ref, all_ref,
    got, sent,
    send_sem, recv_sem, slot_sem, up_sem, side_sem, core_sem, local_sem,
):
    rank = lax.axis_index("ctx")
    planes = n // PLANE
    plane, place = rank // PLANE, rank % PLANE
    side, core = place // 2, place % 2
    right, left = (rank + 1) % n, (rank + n - 1) % n
    above, below = (rank + PLANE) % n, (rank + n - PLANE) % n
    across = plane * PLANE + (1 - side) * 2 + core
    twin = plane * PLANE + side * 2 + (1 - core)
    barrier = pltpu.get_barrier_semaphore()
    for neighbour in (left, right, above, below, across, twin):
        pl.semaphore_signal(barrier, inc=1, device_id={"ctx": neighbour}, device_id_type=MESH)
    pl.semaphore_wait(barrier, 6)
    pieces = got.shape[0]
    splits = pieces // GROUPS
    width = got.shape[2]

    def pass_block(source, slot, sem, target):
        return pltpu.make_async_remote_copy(
            src_ref=source,
            dst_ref=all_ref.at[slot],
            send_sem=sem,
            recv_sem=slot_sem.at[slot],
            device_id={"ctx": target},
            device_id_type=MESH,
        )

    def up(back, source, slot):
        return pass_block(source, slot, up_sem.at[back], above)

    def over(back, source, slot):
        return pass_block(source, slot, side_sem.at[back], across)

    def to_twin(which, source, slot):
        return pass_block(source, slot, core_sem.at[which], twin)

    def keep(which, slot):
        return pltpu.make_async_copy(kv_ref, all_ref.at[slot], local_sem.at[which])

    def arrived(slot):
        pass_block(kv_ref, slot, up_sem.at[0], above).wait_recv()

    def hand_on(piece):
        return pltpu.make_async_remote_copy(
            src_ref=sent.at[piece],
            dst_ref=got.at[piece],
            send_sem=send_sem.at[piece],
            recv_sem=recv_sem.at[piece],
            device_id={"ctx": right},
            device_id_type=MESH,
        )

    def piece_place(piece):
        return piece // splits, slice((piece % splits) * width, (piece % splits + 1) * width)

    near = [back for back in range(1, planes) if back * PLANE + 1 <= reach]

    @pl.when(plane < planes - 1)
    def _():
        up(0, kv_ref, rank).start()

    @pl.when((side == 0) & (plane > 0))
    def _():
        over(0, kv_ref, rank).start()

    @pl.when(core == 0)
    def _():
        to_twin(0, kv_ref, rank).start()
        keep(1, rank + 1).start()

    keep(0, rank).start()

    @pl.when(rank == 0)
    def _():
        for piece in range(pieces):
            group, cols = piece_place(piece)
            sent[piece] = fresh_ref[group, :, cols]
            hand_on(piece).start()
        before_ref[...] = jnp.zeros_like(before_ref)

    def own_across():
        arrived(across)
        to_twin(planes, all_ref.at[across], across).start()

        @pl.when(plane < planes - 1)
        def _():
            up(planes, all_ref.at[across], across).start()

    @pl.when((side == 1) & (plane > 0))
    def _():
        own_across()

    def crosses(back):
        return back in near and back > 1

    for back in range(1, planes):

        @pl.when(plane >= back)
        def _():
            slot = rank - back * PLANE
            arrived(slot)

            @pl.when(plane < planes - 1)
            def _():
                up(back, all_ref.at[slot], slot).start()

            @pl.when((side == 1) | crosses(back))
            def _():
                over(back, all_ref.at[slot], slot).start()

            to_twin(back, all_ref.at[slot], slot).start()

    def take(first, last):
        for piece in range(first, last):
            group, cols = piece_place(piece)
            hand_on(piece).wait_recv()

            @pl.when(rank < n - 1)
            def _():
                sent[piece] = (
                    through_ref[group, 0:1, cols] * got[piece].astype(F32)
                    + fresh_ref[group, :, cols].astype(F32)
                ).astype(BF16)
                hand_on(piece).start()

            before_ref[group, :, cols] = got[piece]

    def below_across():
        for back in range(1, planes):

            @pl.when((plane >= back) & ((side == 0) | (back in near)))
            def _():
                slot = across - back * PLANE
                arrived(slot)
                to_twin(planes + back, all_ref.at[slot], slot).start()

    half = pieces // 2

    @pl.when(rank > 0)
    def _():
        take(0, half)

    @pl.when(plane > 1)
    def _():
        below_across()

    @pl.when(rank > 0)
    def _():
        take(half, pieces)

    @pl.when((side == 0) & (plane == 0))
    def _():
        over(0, kv_ref, rank).start()

    @pl.when((side == 1) & (plane == 0))
    def _():
        own_across()

    @pl.when(plane == 1)
    def _():
        below_across()

    @pl.when(core == 1)
    def _():
        arrived(twin)

    @pl.when(side == 1)
    def _():
        arrived(plane * PLANE + 1 - core)

    for back in range(1, planes):

        @pl.when(plane >= back)
        def _():
            arrived(twin - back * PLANE)

            @pl.when((side == 0) | (back in near))
            def _():
                arrived((plane - back) * PLANE + (1 - side) * 2 + (1 - core))

    @pl.when(rank < n - 1)
    def _():
        for piece in range(pieces):
            hand_on(piece).wait_send()

    @pl.when(plane < planes - 1)
    def _():
        up(0, kv_ref, rank).wait_send()

    @pl.when(side == 0)
    def _():
        over(0, kv_ref, rank).wait_send()

    @pl.when(side == 1)
    def _():
        to_twin(planes, kv_ref, rank).wait_send()

        @pl.when(plane < planes - 1)
        def _():
            up(planes, kv_ref, rank).wait_send()

    @pl.when(core == 0)
    def _():
        to_twin(0, kv_ref, rank).wait_send()
        keep(1, rank + 1).wait()

    keep(0, rank).wait()
    for back in range(1, planes):

        @pl.when(plane >= back)
        def _():
            @pl.when(plane < planes - 1)
            def _():
                up(back, kv_ref, rank).wait_send()

            @pl.when((side == 1) | crosses(back))
            def _():
                over(back, kv_ref, rank).wait_send()

            to_twin(back, kv_ref, rank).wait_send()

            @pl.when((side == 0) | (back in near))
            def _():
                to_twin(planes + back, kv_ref, rank).wait_send()


def mix_kernel(
    docs,
    info_ref,
    x_ref, proj_ref, before_ref, z_ref, gain_ref, skip_ref, step_ref, rate_ref,
    out_ref,
    decay_ref, late_ref, row_ref,
):
    rows = x_ref.shape[0]
    group = pl.program_id(0)
    base = info_ref[0]
    pos = base + lax.broadcasted_iota(jnp.int32, (rows, 1), 0)
    start = start_of(info_ref, pos, docs)

    @pl.when(group == 0)
    def _():
        steps, decay = log_decays(step_ref, rate_ref, rows)
        late = jnp.where(start < base, jnp.exp(decay), 0.0)
        for k in range(GROUPS):
            decay_ref[k] = decay[:, k * PER_GROUP : (k + 1) * PER_GROUP]
            late_ref[k] = late[:, k * PER_GROUP : (k + 1) * PER_GROUP]
        row_ref[...] = (decay - jnp.log(steps)).T

    x = x_ref[...]
    b, c = proj_ref[0, 0], proj_ref[0, 1]
    key_pos = base + lax.broadcasted_iota(jnp.int32, (rows, rows), 1)
    related = (key_pos <= pos) & (key_pos >= start)
    scores = lax.dot_general(c, b, (((1,), (1,)), ((), ())), preferred_element_type=F32)
    scores = jnp.where(related, scores, 0.0)
    columns = decay_ref[group]
    lines = row_ref[pl.ds(pl.multiple_of(group * PER_GROUP, PER_GROUP), PER_GROUP), :]
    lane = lax.broadcasted_iota(jnp.int32, (rows, 2 * HEAD_DIM), 1)
    first = lane < HEAD_DIM
    parts = []
    for pair in range(PER_GROUP // 2):
        weights = []
        for head in (2 * pair, 2 * pair + 1):
            weights.append(
                (
                    scores * jnp.exp(columns[:, head : head + 1] - lines[head : head + 1, :])
                ).astype(BF16)
            )
        own = x[:, pair * 2 * HEAD_DIM : (pair + 1) * 2 * HEAD_DIM]
        zero = jnp.zeros_like(own)
        stacked = jnp.concatenate([jnp.where(first, own, zero), jnp.where(first, zero, own)], axis=0)
        parts.append(
            jnp.dot(jnp.concatenate(weights, axis=1), stacked, preferred_element_type=F32)
        )
    inner = jnp.concatenate(parts, axis=1)
    carried = jnp.dot(c, before_ref[0], preferred_element_type=F32)
    mixed = inner + carried * spread_heads(late_ref[group]) + skip_ref[...] * x.astype(F32)
    z = z_ref[...].astype(F32)
    gated = mixed * (z * jax.nn.sigmoid(z))
    scaling = lax.rsqrt(jnp.mean(gated * gated, axis=1, keepdims=True) + EPSILON)
    out_ref[...] = (gated * scaling * gain_ref[...]).astype(BF16)


def attend_kernel(docs, step_rows, info_ref, q_ref, k_ref, v_ref, out_ref, bias_ref):
    rows = q_ref.shape[0]
    group_size = q_ref.shape[1] // QDIM
    base = info_ref[0]
    earliest = jnp.int32(0)
    for doc in range(1, docs):
        earliest = jnp.where(base >= info_ref[1 + doc], info_ref[1 + doc], earliest)
    first_block = lax.div(earliest, step_rows)
    last_block = lax.div(base + rows - 1, step_rows) + 1
    factor = QDIM ** (-0.5) * 1.4426950408889634

    @pl.when(pl.program_id(0) == 0)
    def _():
        pos = base + lax.broadcasted_iota(jnp.int32, (rows, 1), 0)
        start = start_of(info_ref, pos, docs)

        def fill(block, carry):
            key_pos = block * step_rows + lax.broadcasted_iota(jnp.int32, (rows, step_rows), 1)
            visible = (key_pos <= pos) & (key_pos >= start)
            bias_ref[block] = jnp.where(visible, 0.0, NEGATIVE)
            return carry

        lax.fori_loop(first_block, last_block, fill, 0)

    halves = 2
    each = group_size // halves
    tall = rows * each
    qs = [
        jnp.concatenate(
            [q_ref[:, i * QDIM : (i + 1) * QDIM] for i in range(h * each, (h + 1) * each)], axis=0
        )
        for h in range(halves)
    ]

    def step(block, carry):
        offset = pl.multiple_of(block * step_rows, step_rows)
        keys = k_ref[pl.ds(offset, step_rows), :]
        values = v_ref[pl.ds(offset, step_rows), :]
        wide = jnp.concatenate([values, jnp.ones_like(values)], axis=1)
        bias = jnp.concatenate([bias_ref[block]] * each, axis=0)
        scores = [
            lax.dot_general(q, keys, (((1,), (1,)), ((), ())), preferred_element_type=F32) + bias
            for q in qs
        ]
        result = []
        for h in range(halves):
            high, accum = carry[h]
            high_next = jnp.maximum(high, jnp.max(scores[h], axis=1, keepdims=True))
            numerators = jnp.exp2((scores[h] - high_next) * factor).astype(BF16)
            fading = jnp.exp2((high - high_next) * factor)
            result.append(
                (
                    high_next,
                    accum * fading + jnp.dot(numerators, wide, preferred_element_type=F32),
                )
            )
        return tuple(result)

    initial = (jnp.full((tall, 1), NEGATIVE, F32), jnp.zeros((tall, 2 * QDIM), F32))
    final = lax.fori_loop(first_block, last_block, step, (initial,) * halves)
    for h in range(halves):
        accum = final[h][1]
        result = (accum[:, :QDIM] / accum[:, QDIM:]).astype(BF16)
        for i in range(each):
            col = (h * each + i) * QDIM
            out_ref[:, col : col + QDIM] = result[i * rows : (i + 1) * rows, :]


def params(limit, **more):
    return pltpu.CompilerParams(vmem_limit_bytes=limit * 2**20, **more)


def on_device(
    mixer_input,
    z_gate,
    time_step,
    conv_weight,
    conv_bias,
    decay_rate,
    skip_gain,
    norm_gain,
    doc_lengths,
    queries,
    attn_keys,
    attn_values,
):
    rows = mixer_input.shape[1]
    width = mixer_input.shape[2]
    inner_width = HEADS * HEAD_DIM
    docs = doc_lengths.shape[1]
    taps = conv_weight.shape[0]
    n = lax.axis_size("ctx")
    rank = lax.axis_index("ctx")
    own_kv = jnp.concatenate([attn_keys[0], attn_values[0]], axis=1)
    rim = lax.ppermute(
        mixer_input[0, rows - RIM :, :], "ctx", [(i, i + 1) for i in range(n - 1)]
    )
    lengths = lax.dynamic_slice_in_dim(doc_lengths, lax.axis_index("batch"), 1, 0)[0]
    info = jnp.concatenate([(rank * rows).astype(jnp.int32)[None], jnp.cumsum(lengths) - lengths])
    rates = decay_rate[None]
    bias = conv_bias[None]
    skips = jnp.repeat(skip_gain, HEAD_DIM)[None]
    first_b = inner_width // STATE
    first_c = first_b + GROUPS
    smem = pl.BlockSpec(memory_space=pltpu.SMEM)

    def wide(height):
        return pl.BlockSpec((height, GROUP_WIDTH), lambda g: (0, g))

    def narrow(height, first):
        return pl.BlockSpec((height, STATE), lambda g: (0, first + g))

    def trio(height):
        return [wide(height), narrow(height, first_b), narrow(height, first_c)]

    whole = pl.BlockSpec((rows, HEADS), lambda g: (0, 0))
    rate_spec = pl.BlockSpec((1, HEADS), lambda g: (0, 0))
    per_group = lambda *shape: pl.BlockSpec((1,) + shape, lambda g: (g,) + (0,) * len(shape))
    inputs = mixer_input[0]
    act, proj, fresh, through = pl.pallas_call(
        functools.partial(fresh_kernel, docs),
        grid=(GROUPS,),
        in_specs=[smem] + trio(rows) + trio(RIM) + trio(taps) + trio(1) + [whole, rate_spec],
        out_specs=[
            wide(rows),
            per_group(2, rows, STATE),
            per_group(STATE, GROUP_WIDTH),
            per_group(8, GROUP_WIDTH),
        ],
        out_shape=[
            jax.ShapeDtypeStruct((rows, inner_width), BF16),
            jax.ShapeDtypeStruct((GROUPS, 2, rows, STATE), BF16),
            jax.ShapeDtypeStruct((GROUPS, STATE, GROUP_WIDTH), BF16),
            jax.ShapeDtypeStruct((GROUPS, 8, GROUP_WIDTH), F32),
        ],
        scratch_shapes=[
            pltpu.VMEM((8 + rows, GROUP_WIDTH), F32),
            pltpu.VMEM((GROUPS, rows, PER_GROUP), F32),
            pltpu.VMEM((GROUPS, 8, PER_GROUP), F32),
        ],
        compiler_params=params(24),
        cost_estimate=pl.CostEstimate(
            flops=6 * 10**8, bytes_accessed=8 * 10**6, transcendentals=10**6
        ),
        name="fresh_states",
    )(
        info,
        inputs, inputs, inputs,
        rim, rim, rim,
        conv_weight, conv_weight, conv_weight,
        bias, bias, bias,
        time_step[0],
        rates,
    )

    pieces = 4 * GROUPS
    piece_width = GROUPS * GROUP_WIDTH // pieces
    vmem = pl.BlockSpec(memory_space=pltpu.VMEM)
    anywhere = pl.BlockSpec(memory_space=pl.ANY)
    before, all_kv = pl.pallas_call(
        functools.partial(chain_kernel, n, -(-(MOST - 1) // rows)),
        in_specs=[vmem, vmem, anywhere],
        out_specs=[vmem, anywhere],
        out_shape=[
            jax.ShapeDtypeStruct((GROUPS, STATE, GROUP_WIDTH), BF16),
            jax.ShapeDtypeStruct((n,) + own_kv.shape, BF16),
        ],
        scratch_shapes=[
            pltpu.VMEM((pieces, STATE, piece_width), BF16),
            pltpu.VMEM((pieces, STATE, piece_width), BF16),
            pltpu.SemaphoreType.DMA((pieces,)),
            pltpu.SemaphoreType.DMA((pieces,)),
            pltpu.SemaphoreType.DMA((n,)),
            pltpu.SemaphoreType.DMA((n // PLANE + 1,)),
            pltpu.SemaphoreType.DMA((n // PLANE,)),
            pltpu.SemaphoreType.DMA((2 * n // PLANE,)),
            pltpu.SemaphoreType.DMA((2,)),
        ],
        compiler_params=params(24, collective_id=0, has_side_effects=True),
        cost_estimate=pl.CostEstimate(
            flops=10**7, bytes_accessed=2 * 10**8, transcendentals=0
        ),
        name="hand_on_states",
    )(fresh, through, own_kv)

    mixer_out = pl.pallas_call(
        functools.partial(mix_kernel, docs),
        grid=(GROUPS,),
        in_specs=[
            smem,
            wide(rows),
            per_group(2, rows, STATE),
            per_group(STATE, GROUP_WIDTH),
            wide(rows),
            wide(1),
            wide(1),
            whole,
            rate_spec,
        ],
        out_specs=wide(rows),
        out_shape=jax.ShapeDtypeStruct((rows, inner_width), BF16),
        scratch_shapes=[
            pltpu.VMEM((GROUPS, rows, PER_GROUP), F32),
            pltpu.VMEM((GROUPS, rows, PER_GROUP), F32),
            pltpu.VMEM((HEADS, rows), F32),
        ],
        compiler_params=params(24),
        cost_estimate=pl.CostEstimate(
            flops=10**9, bytes_accessed=10**7, transcendentals=4 * 10**6
        ),
        name="mix_heads",
    )(info, act, proj, before, z_gate[0], norm_gain[None], skips, time_step[0], rates)

    seq_len = n * rows
    all_kv = all_kv.reshape(seq_len, own_kv.shape[1])
    q_width = queries.shape[2] // KVHEADS
    step_rows = 256
    attn_out = pl.pallas_call(
        functools.partial(attend_kernel, docs, step_rows),
        grid=(KVHEADS,),
        in_specs=[
            smem,
            pl.BlockSpec((rows, q_width), lambda g: (0, g)),
            pl.BlockSpec((seq_len, QDIM), lambda g: (0, g)),
            pl.BlockSpec((seq_len, QDIM), lambda g: (0, KVHEADS + g)),
        ],
        out_specs=pl.BlockSpec((rows, q_width), lambda g: (0, g)),
        out_shape=jax.ShapeDtypeStruct((rows, QHEADS * QDIM), BF16),
        scratch_shapes=[pltpu.VMEM((seq_len // step_rows, rows, step_rows), F32)],
        compiler_params=params(24),
        cost_estimate=pl.CostEstimate(
            flops=4 * 10**9, bytes_accessed=10**7, transcendentals=8 * 10**6
        ),
        name="attend",
    )(info, queries[0], all_kv, all_kv)
    return (mixer_out[None], attn_out[None])


def solution(mesh):
    spread = P("batch", "ctx", None)
    placed = (spread,) * 3 + (P(),) * 6 + (spread,) * 3
    return jax.shard_map(
        on_device,
        mesh=mesh,
        in_specs=placed,
        out_specs=(spread, spread),
        check_vma=False,
    )
```

```python
import functools

import jax
import jax.numpy as jnp
from jax import lax
from jax.experimental import pallas as pl
from jax.experimental.pallas import tpu as pltpu
from jax.sharding import PartitionSpec as P

HEADS = 128
HEAD_DIM = 64
STATE = 128
GROUPS = 8
QHEADS = 32
KVHEADS = 8
QDIM = 128
PER_GROUP = HEADS // GROUPS
GROUP_WIDTH = PER_GROUP * HEAD_DIM
RIM = 16
MOST = 1536
PLANE = 4

EPSILON = 1e-05
NEGATIVE = -1e30
F32 = jnp.float32
BF16 = jnp.bfloat16
MESH = pl.DeviceIdType.MESH


def start_of(info_ref, positions, docs):
    start = jnp.zeros_like(positions)
    for doc in range(1, docs):
        first = info_ref[1 + doc]
        start = jnp.where(positions >= first, first, start)
    return start


def log_decays(step_ref, rate_ref, rows):
    steps = jax.nn.softplus(step_ref[...].astype(F32))
    fall = -steps * rate_ref[...]
    lower = (
        lax.broadcasted_iota(jnp.int32, (rows, rows), 0)
        >= lax.broadcasted_iota(jnp.int32, (rows, rows), 1)
    ).astype(F32)
    return steps, jnp.dot(
        lower, fall, precision=lax.Precision.HIGHEST, preferred_element_type=F32
    )


def spread_heads(per_head):
    high = per_head.astype(BF16)
    low = (per_head - high.astype(F32)).astype(BF16)
    both = jnp.concatenate([high, low], axis=1)
    row = lax.broadcasted_iota(jnp.int32, (2 * PER_GROUP, GROUP_WIDTH), 0)
    col = lax.broadcasted_iota(jnp.int32, (2 * PER_GROUP, GROUP_WIDTH), 1)
    own = (lax.rem(row, PER_GROUP) == lax.div(col, HEAD_DIM)).astype(BF16)
    return jnp.dot(both, own, preferred_element_type=F32)


def conv_silu(in_ref, rim_ref, weight_ref, bias_ref, pad_ref, same):
    rows, width = in_ref.shape
    pad_ref[0:8, 0:width] = rim_ref[8:16, :].astype(F32)
    pad_ref[8 : 8 + rows, 0:width] = in_ref[...].astype(F32)
    taps = weight_ref.shape[0]
    summed = pad_ref[8 : 8 + rows, 0:width] * weight_ref[taps - 1 : taps, :] + bias_ref[...]
    for back in range(1, taps):
        window = pad_ref[8 - back : 8 - back + rows, 0:width]
        tap = weight_ref[taps - 1 - back : taps - back, :]
        summed = summed + jnp.where(same[back - 1], window * tap, 0.0)
    return (summed * jax.nn.sigmoid(summed)).astype(BF16)


def fresh_kernel(
    docs,
    info_ref,
    x_ref, b_ref, c_ref,
    rim_x_ref, rim_b_ref, rim_c_ref,
    w_x_ref, w_b_ref, w_c_ref,
    o_x_ref, o_b_ref, o_c_ref,
    step_ref, rate_ref,
    act_ref, proj_ref, fresh_ref, through_ref,
    pad_ref, trail_ref, last_ref,
):
    rows = x_ref.shape[0]
    group = pl.program_id(0)
    base = info_ref[0]
    pos = base + lax.broadcasted_iota(jnp.int32, (rows, 1), 0)
    start = start_of(info_ref, pos, docs)

    @pl.when(group == 0)
    def _():
        steps, decay = log_decays(step_ref, rate_ref, rows)
        last_pos = jnp.full((rows, 1), base + rows - 1, jnp.int32)
        last_start = start_of(info_ref, last_pos, docs)
        final = decay[rows - 1 : rows, :]
        trail = jnp.where(pos >= last_start, jnp.exp(final - decay) * steps, 0.0)
        carry = jnp.where(
            last_start[0:8] < base, jnp.exp(jnp.broadcast_to(final, (8, HEADS))), 0.0
        )
        for k in range(GROUPS):
            trail_ref[k] = trail[:, k * PER_GROUP : (k + 1) * PER_GROUP]
            last_ref[k] = carry[:, k * PER_GROUP : (k + 1) * PER_GROUP]

    same = [pos - back >= start for back in range(1, w_x_ref.shape[0])]
    x = conv_silu(x_ref, rim_x_ref, w_x_ref, o_x_ref, pad_ref, same)
    b = conv_silu(b_ref, rim_b_ref, w_b_ref, o_b_ref, pad_ref, same)
    c = conv_silu(c_ref, rim_c_ref, w_c_ref, o_c_ref, pad_ref, same)
    act_ref[...] = x
    proj_ref[0, 0] = b
    proj_ref[0, 1] = c
    scaled = (x.astype(F32) * spread_heads(trail_ref[group])).astype(BF16)
    fresh_ref[0] = lax.dot_general(
        b, scaled, (((0,), (0,)), ((), ())), preferred_element_type=F32
    ).astype(BF16)
    through_ref[0] = spread_heads(last_ref[group])


def chain_kernel(
    n,
    reach,
    fresh_ref, through_ref, kv_ref,
    before_ref, all_ref,
    got, sent,
    send_sem, recv_sem, slot_sem, up_sem, side_sem, core_sem, local_sem,
):
    rank = lax.axis_index("ctx")
    planes = n // PLANE
    plane, place = rank // PLANE, rank % PLANE
    side, core = place // 2, place % 2
    right, left = (rank + 1) % n, (rank + n - 1) % n
    above, below = (rank + PLANE) % n, (rank + n - PLANE) % n
    across = plane * PLANE + (1 - side) * 2 + core
    twin = plane * PLANE + side * 2 + (1 - core)
    barrier = pltpu.get_barrier_semaphore()
    for neighbour in (left, right, above, below, across, twin):
        pl.semaphore_signal(barrier, inc=1, device_id={"ctx": neighbour}, device_id_type=MESH)
    pl.semaphore_wait(barrier, 6)
    pieces = got.shape[0]
    splits = pieces // GROUPS
    width = got.shape[2]

    def pass_block(source, slot, sem, target):
        return pltpu.make_async_remote_copy(
            src_ref=source,
            dst_ref=all_ref.at[slot],
            send_sem=sem,
            recv_sem=slot_sem.at[slot],
            device_id={"ctx": target},
            device_id_type=MESH,
        )

    def up(back, source, slot):
        return pass_block(source, slot, up_sem.at[back], above)

    def over(back, source, slot):
        return pass_block(source, slot, side_sem.at[back], across)

    def to_twin(which, source, slot):
        return pass_block(source, slot, core_sem.at[which], twin)

    def keep(which, slot):
        return pltpu.make_async_copy(kv_ref, all_ref.at[slot], local_sem.at[which])

    def arrived(slot):
        pass_block(kv_ref, slot, up_sem.at[0], above).wait_recv()

    def hand_on(piece):
        return pltpu.make_async_remote_copy(
            src_ref=sent.at[piece],
            dst_ref=got.at[piece],
            send_sem=send_sem.at[piece],
            recv_sem=recv_sem.at[piece],
            device_id={"ctx": right},
            device_id_type=MESH,
        )

    def piece_place(piece):
        return piece // splits, slice((piece % splits) * width, (piece % splits + 1) * width)

    near = [back for back in range(1, planes) if back * PLANE + 1 <= reach]

    @pl.when(plane < planes - 1)
    def _():
        up(0, kv_ref, rank).start()

    @pl.when((side == 0) & (plane > 0))
    def _():
        over(0, kv_ref, rank).start()

    @pl.when(core == 0)
    def _():
        to_twin(0, kv_ref, rank).start()
        keep(1, rank + 1).start()

    keep(0, rank).start()

    @pl.when(rank == 0)
    def _():
        for piece in range(pieces):
            group, cols = piece_place(piece)
            sent[piece] = fresh_ref[group, :, cols]
            hand_on(piece).start()
        before_ref[...] = jnp.zeros_like(before_ref)

    def own_across():
        arrived(across)
        to_twin(planes, all_ref.at[across], across).start()

    def crosses(back):
        return back in near

    for back in range(1, planes):

        @pl.when(plane >= back)
        def _():
            slot = rank - back * PLANE
            arrived(slot)

            @pl.when(plane < planes - 1)
            def _():
                up(back, all_ref.at[slot], slot).start()

            @pl.when((side == 1) | crosses(back))
            def _():
                over(back, all_ref.at[slot], slot).start()

            to_twin(back, all_ref.at[slot], slot).start()

    def take(first, last):
        for piece in range(first, last):
            group, cols = piece_place(piece)
            hand_on(piece).wait_recv()

            @pl.when(rank < n - 1)
            def _():
                sent[piece] = (
                    through_ref[group, 0:1, cols] * got[piece].astype(F32)
                    + fresh_ref[group, :, cols].astype(F32)
                ).astype(BF16)
                hand_on(piece).start()

            before_ref[group, :, cols] = got[piece]

    def below_across():
        for back in range(1, planes):

            @pl.when((plane >= back) & ((side == 0) | (back in near)))
            def _():
                slot = across - back * PLANE
                arrived(slot)
                to_twin(planes + back, all_ref.at[slot], slot).start()

    most = pieces * 3 // 4

    @pl.when(rank > 0)
    def _():
        take(0, most)

    @pl.when(plane == planes - 1)
    def _():
        below_across()

    @pl.when(rank > 0)
    def _():
        take(most, pieces)

    @pl.when((side == 0) & (plane == 0))
    def _():
        over(0, kv_ref, rank).start()

    @pl.when(side == 1)
    def _():
        own_across()

    @pl.when(plane < planes - 1)
    def _():
        below_across()

    @pl.when(core == 1)
    def _():
        arrived(twin)

    @pl.when(side == 1)
    def _():
        arrived(plane * PLANE + 1 - core)

    for back in range(1, planes):

        @pl.when(plane >= back)
        def _():
            arrived(twin - back * PLANE)

            @pl.when((side == 0) | (back in near))
            def _():
                arrived((plane - back) * PLANE + (1 - side) * 2 + (1 - core))

    @pl.when(rank < n - 1)
    def _():
        for piece in range(pieces):
            hand_on(piece).wait_send()

    @pl.when(plane < planes - 1)
    def _():
        up(0, kv_ref, rank).wait_send()

    @pl.when(side == 0)
    def _():
        over(0, kv_ref, rank).wait_send()

    @pl.when(side == 1)
    def _():
        to_twin(planes, kv_ref, rank).wait_send()

    @pl.when(core == 0)
    def _():
        to_twin(0, kv_ref, rank).wait_send()
        keep(1, rank + 1).wait()

    keep(0, rank).wait()
    for back in range(1, planes):

        @pl.when(plane >= back)
        def _():
            @pl.when(plane < planes - 1)
            def _():
                up(back, kv_ref, rank).wait_send()

            @pl.when((side == 1) | crosses(back))
            def _():
                over(back, kv_ref, rank).wait_send()

            to_twin(back, kv_ref, rank).wait_send()

            @pl.when((side == 0) | (back in near))
            def _():
                to_twin(planes + back, kv_ref, rank).wait_send()


def mix_kernel(
    docs,
    info_ref,
    x_ref, proj_ref, before_ref, z_ref, gain_ref, skip_ref, step_ref, rate_ref,
    out_ref,
    decay_ref, late_ref, row_ref,
):
    rows = x_ref.shape[0]
    group = pl.program_id(0)
    base = info_ref[0]
    pos = base + lax.broadcasted_iota(jnp.int32, (rows, 1), 0)
    start = start_of(info_ref, pos, docs)

    @pl.when(group == 0)
    def _():
        steps, decay = log_decays(step_ref, rate_ref, rows)
        late = jnp.where(start < base, jnp.exp(decay), 0.0)
        for k in range(GROUPS):
            decay_ref[k] = decay[:, k * PER_GROUP : (k + 1) * PER_GROUP]
            late_ref[k] = late[:, k * PER_GROUP : (k + 1) * PER_GROUP]
        row_ref[...] = (decay - jnp.log(steps)).T

    x = x_ref[...]
    b, c = proj_ref[0, 0], proj_ref[0, 1]
    key_pos = base + lax.broadcasted_iota(jnp.int32, (rows, rows), 1)
    related = (key_pos <= pos) & (key_pos >= start)
    scores = lax.dot_general(c, b, (((1,), (1,)), ((), ())), preferred_element_type=F32)
    scores = jnp.where(related, scores, 0.0)
    columns = decay_ref[group]
    lines = row_ref[pl.ds(pl.multiple_of(group * PER_GROUP, PER_GROUP), PER_GROUP), :]
    lane = lax.broadcasted_iota(jnp.int32, (rows, 2 * HEAD_DIM), 1)
    first = lane < HEAD_DIM
    parts = []
    for pair in range(PER_GROUP // 2):
        weights = []
        for head in (2 * pair, 2 * pair + 1):
            weights.append(
                (
                    scores * jnp.exp(columns[:, head : head + 1] - lines[head : head + 1, :])
                ).astype(BF16)
            )
        own = x[:, pair * 2 * HEAD_DIM : (pair + 1) * 2 * HEAD_DIM]
        zero = jnp.zeros_like(own)
        stacked = jnp.concatenate([jnp.where(first, own, zero), jnp.where(first, zero, own)], axis=0)
        parts.append(
            jnp.dot(jnp.concatenate(weights, axis=1), stacked, preferred_element_type=F32)
        )
    inner = jnp.concatenate(parts, axis=1)
    carried = jnp.dot(c, before_ref[0], preferred_element_type=F32)
    mixed = inner + carried * spread_heads(late_ref[group]) + skip_ref[...] * x.astype(F32)
    z = z_ref[...].astype(F32)
    gated = mixed * (z * jax.nn.sigmoid(z))
    scaling = lax.rsqrt(jnp.mean(gated * gated, axis=1, keepdims=True) + EPSILON)
    out_ref[...] = (gated * scaling * gain_ref[...]).astype(BF16)


def attend_kernel(docs, step_rows, info_ref, q_ref, k_ref, v_ref, out_ref, bias_ref):
    rows = q_ref.shape[0]
    group_size = q_ref.shape[1] // QDIM
    base = info_ref[0]
    earliest = jnp.int32(0)
    for doc in range(1, docs):
        earliest = jnp.where(base >= info_ref[1 + doc], info_ref[1 + doc], earliest)
    first_block = lax.div(earliest, step_rows)
    last_block = lax.div(base + rows - 1, step_rows) + 1
    factor = QDIM ** (-0.5) * 1.4426950408889634

    @pl.when(pl.program_id(0) == 0)
    def _():
        pos = base + lax.broadcasted_iota(jnp.int32, (rows, 1), 0)
        start = start_of(info_ref, pos, docs)

        def fill(block, carry):
            key_pos = block * step_rows + lax.broadcasted_iota(jnp.int32, (rows, step_rows), 1)
            visible = (key_pos <= pos) & (key_pos >= start)
            bias_ref[block] = jnp.where(visible, 0.0, NEGATIVE)
            return carry

        lax.fori_loop(first_block, last_block, fill, 0)

    halves = 2
    each = group_size // halves
    tall = rows * each
    qs = [
        jnp.concatenate(
            [q_ref[:, i * QDIM : (i + 1) * QDIM] for i in range(h * each, (h + 1) * each)], axis=0
        )
        for h in range(halves)
    ]

    def step(block, carry):
        offset = pl.multiple_of(block * step_rows, step_rows)
        keys = k_ref[pl.ds(offset, step_rows), :]
        values = v_ref[pl.ds(offset, step_rows), :]
        wide = jnp.concatenate([values, jnp.ones_like(values)], axis=1)
        bias = jnp.concatenate([bias_ref[block]] * each, axis=0)
        scores = [
            lax.dot_general(q, keys, (((1,), (1,)), ((), ())), preferred_element_type=F32) + bias
            for q in qs
        ]
        result = []
        for h in range(halves):
            high, accum = carry[h]
            high_next = jnp.maximum(high, jnp.max(scores[h], axis=1, keepdims=True))
            numerators = jnp.exp2((scores[h] - high_next) * factor).astype(BF16)
            fading = jnp.exp2((high - high_next) * factor)
            result.append(
                (
                    high_next,
                    accum * fading + jnp.dot(numerators, wide, preferred_element_type=F32),
                )
            )
        return tuple(result)

    initial = (jnp.full((tall, 1), NEGATIVE, F32), jnp.zeros((tall, 2 * QDIM), F32))
    final = lax.fori_loop(first_block, last_block, step, (initial,) * halves)
    for h in range(halves):
        accum = final[h][1]
        result = (accum[:, :QDIM] / accum[:, QDIM:]).astype(BF16)
        for i in range(each):
            col = (h * each + i) * QDIM
            out_ref[:, col : col + QDIM] = result[i * rows : (i + 1) * rows, :]


def params(limit, **more):
    return pltpu.CompilerParams(vmem_limit_bytes=limit * 2**20, **more)


def on_device(
    mixer_input,
    z_gate,
    time_step,
    conv_weight,
    conv_bias,
    decay_rate,
    skip_gain,
    norm_gain,
    doc_lengths,
    queries,
    attn_keys,
    attn_values,
):
    rows = mixer_input.shape[1]
    width = mixer_input.shape[2]
    inner_width = HEADS * HEAD_DIM
    docs = doc_lengths.shape[1]
    taps = conv_weight.shape[0]
    n = lax.axis_size("ctx")
    rank = lax.axis_index("ctx")
    own_kv = jnp.concatenate([attn_keys[0], attn_values[0]], axis=1)
    rim = lax.ppermute(
        mixer_input[0, rows - RIM :, :], "ctx", [(i, i + 1) for i in range(n - 1)]
    )
    lengths = lax.dynamic_slice_in_dim(doc_lengths, lax.axis_index("batch"), 1, 0)[0]
    info = jnp.concatenate([(rank * rows).astype(jnp.int32)[None], jnp.cumsum(lengths) - lengths])
    rates = decay_rate[None]
    bias = conv_bias[None]
    skips = jnp.repeat(skip_gain, HEAD_DIM)[None]
    first_b = inner_width // STATE
    first_c = first_b + GROUPS
    smem = pl.BlockSpec(memory_space=pltpu.SMEM)

    def wide(height):
        return pl.BlockSpec((height, GROUP_WIDTH), lambda g: (0, g))

    def narrow(height, first):
        return pl.BlockSpec((height, STATE), lambda g: (0, first + g))

    def trio(height):
        return [wide(height), narrow(height, first_b), narrow(height, first_c)]

    whole = pl.BlockSpec((rows, HEADS), lambda g: (0, 0))
    rate_spec = pl.BlockSpec((1, HEADS), lambda g: (0, 0))
    per_group = lambda *shape: pl.BlockSpec((1,) + shape, lambda g: (g,) + (0,) * len(shape))
    inputs = mixer_input[0]
    act, proj, fresh, through = pl.pallas_call(
        functools.partial(fresh_kernel, docs),
        grid=(GROUPS,),
        in_specs=[smem] + trio(rows) + trio(RIM) + trio(taps) + trio(1) + [whole, rate_spec],
        out_specs=[
            wide(rows),
            per_group(2, rows, STATE),
            per_group(STATE, GROUP_WIDTH),
            per_group(8, GROUP_WIDTH),
        ],
        out_shape=[
            jax.ShapeDtypeStruct((rows, inner_width), BF16),
            jax.ShapeDtypeStruct((GROUPS, 2, rows, STATE), BF16),
            jax.ShapeDtypeStruct((GROUPS, STATE, GROUP_WIDTH), BF16),
            jax.ShapeDtypeStruct((GROUPS, 8, GROUP_WIDTH), F32),
        ],
        scratch_shapes=[
            pltpu.VMEM((8 + rows, GROUP_WIDTH), F32),
            pltpu.VMEM((GROUPS, rows, PER_GROUP), F32),
            pltpu.VMEM((GROUPS, 8, PER_GROUP), F32),
        ],
        compiler_params=params(24),
        cost_estimate=pl.CostEstimate(
            flops=6 * 10**8, bytes_accessed=8 * 10**6, transcendentals=10**6
        ),
        name="fresh_states",
    )(
        info,
        inputs, inputs, inputs,
        rim, rim, rim,
        conv_weight, conv_weight, conv_weight,
        bias, bias, bias,
        time_step[0],
        rates,
    )

    pieces = 2 * GROUPS
    piece_width = GROUPS * GROUP_WIDTH // pieces
    vmem = pl.BlockSpec(memory_space=pltpu.VMEM)
    anywhere = pl.BlockSpec(memory_space=pl.ANY)
    before, all_kv = pl.pallas_call(
        functools.partial(chain_kernel, n, -(-(MOST - 1) // rows)),
        in_specs=[vmem, vmem, anywhere],
        out_specs=[vmem, anywhere],
        out_shape=[
            jax.ShapeDtypeStruct((GROUPS, STATE, GROUP_WIDTH), BF16),
            jax.ShapeDtypeStruct((n,) + own_kv.shape, BF16),
        ],
        scratch_shapes=[
            pltpu.VMEM((pieces, STATE, piece_width), BF16),
            pltpu.VMEM((pieces, STATE, piece_width), BF16),
            pltpu.SemaphoreType.DMA((pieces,)),
            pltpu.SemaphoreType.DMA((pieces,)),
            pltpu.SemaphoreType.DMA((n,)),
            pltpu.SemaphoreType.DMA((n // PLANE,)),
            pltpu.SemaphoreType.DMA((n // PLANE,)),
            pltpu.SemaphoreType.DMA((2 * n // PLANE,)),
            pltpu.SemaphoreType.DMA((2,)),
        ],
        compiler_params=params(24, collective_id=0, has_side_effects=True),
        cost_estimate=pl.CostEstimate(
            flops=10**7, bytes_accessed=2 * 10**8, transcendentals=0
        ),
        name="hand_on_states",
    )(fresh, through, own_kv)

    mixer_out = pl.pallas_call(
        functools.partial(mix_kernel, docs),
        grid=(GROUPS,),
        in_specs=[
            smem,
            wide(rows),
            per_group(2, rows, STATE),
            per_group(STATE, GROUP_WIDTH),
            wide(rows),
            wide(1),
            wide(1),
            whole,
            rate_spec,
        ],
        out_specs=wide(rows),
        out_shape=jax.ShapeDtypeStruct((rows, inner_width), BF16),
        scratch_shapes=[
            pltpu.VMEM((GROUPS, rows, PER_GROUP), F32),
            pltpu.VMEM((GROUPS, rows, PER_GROUP), F32),
            pltpu.VMEM((HEADS, rows), F32),
        ],
        compiler_params=params(24),
        cost_estimate=pl.CostEstimate(
            flops=10**9, bytes_accessed=10**7, transcendentals=4 * 10**6
        ),
        name="mix_heads",
    )(info, act, proj, before, z_gate[0], norm_gain[None], skips, time_step[0], rates)

    seq_len = n * rows
    all_kv = all_kv.reshape(seq_len, own_kv.shape[1])
    q_width = queries.shape[2] // KVHEADS
    step_rows = 256
    attn_out = pl.pallas_call(
        functools.partial(attend_kernel, docs, step_rows),
        grid=(KVHEADS,),
        in_specs=[
            smem,
            pl.BlockSpec((rows, q_width), lambda g: (0, g)),
            pl.BlockSpec((seq_len, QDIM), lambda g: (0, g)),
            pl.BlockSpec((seq_len, QDIM), lambda g: (0, KVHEADS + g)),
        ],
        out_specs=pl.BlockSpec((rows, q_width), lambda g: (0, g)),
        out_shape=jax.ShapeDtypeStruct((rows, QHEADS * QDIM), BF16),
        scratch_shapes=[pltpu.VMEM((seq_len // step_rows, rows, step_rows), F32)],
        compiler_params=params(24),
        cost_estimate=pl.CostEstimate(
            flops=4 * 10**9, bytes_accessed=10**7, transcendentals=8 * 10**6
        ),
        name="attend",
    )(info, queries[0], all_kv, all_kv)
    return (mixer_out[None], attn_out[None])


def solution(mesh):
    spread = P("batch", "ctx", None)
    placed = (spread,) * 3 + (P(),) * 6 + (spread,) * 3
    return jax.shard_map(
        on_device,
        mesh=mesh,
        in_specs=placed,
        out_specs=(spread, spread),
        check_vma=False,
    )
```
